128 devices in a mesh: row: 16 (over y, x), col: 8 (over z, core).
Axes of the slice: x: 4, y: 4, z: 4, core: 2. Of those that a mesh axis runs over, the one named last changes fastest.
Arguments:
- alignment_features: bfloat16 [1024, 1024, 256], P(('row', 'col')), may hold values from -6 to 6
- standardize_gain: float32 [256], replicated, may hold values from 0.25 to 1.75
- standardize_offset: float32 [256], replicated, may hold values from -3 to 3
- first_factor_matrix: bfloat16 [256, 32], replicated, may hold values from -0.375 to 0.375
- first_factor_offset: float32 [32], replicated, may hold values from -3 to 3
- second_factor_matrix: bfloat16 [256, 32], replicated, may hold values from -0.375 to 0.375
- second_factor_offset: float32 [32], replicated, may hold values from -3 to 3
- final_matrix: bfloat16 [1024, 128], replicated, may hold values from -1 to 1
- final_offset: float32 [128], replicated, may hold values from -3 to 3
- pairwise_features: bfloat16 [1024, 1024, 128], P('row', 'col'), may hold values from -6 to 6
Outputs:
- pair_out: bfloat16 [1024, 1024, 128], P('row', 'col')
The draws below stay inside these ranges and needn't reach their ends.
All inputs are finite; a program needn't handle non-finite values.
Results may differ from the reference program's by a relative error of at most 0.005.
Values may be sent and summed in bfloat16 or wider, within the bound.
No kernel may reach another device: no remote copies, remote signals or barrier semaphores. Data moves between devices by JAX's collectives and lax.ppermute only.
A program may use at most 192 MiB of HBM per device.

```python
import jax
import jax.numpy as jnp
from jax import lax

ALIGNMENT_WIDTH = 256
FACTOR_DEPTH = 32
PAIR = 128
CHAIN_LENGTH = 1024
ALIGNMENT_DEPTH = 1024


def levels(own_key, shape, pieces, least, top_value):
    level = 1.0
    for dim, blocks in pieces:
        heights = jax.random.uniform(jax.random.fold_in(jax.random.fold_in(own_key, 6), dim), (blocks,), jnp.float32, least / len(pieces), top_value / len(pieces))
        level = level * jnp.repeat(jnp.exp(heights), shape[dim] // blocks).reshape((-1,) + (1,) * (len(shape) - 1 - dim))
    return level


def normal_values(key, dims, spread, reach, split=(), kind=jnp.bfloat16):
    gain = levels(key, dims, split, -0.22, 0.18) if split else 1.0
    entries = jax.random.normal(key, dims, jnp.float32) * spread * gain
    return jnp.minimum(jnp.maximum(entries, -reach), reach).astype(kind)


def setup_inputs(seed: int = 0) -> dict:
    arg_keys = jax.random.split(jax.random.key(seed), 11)
    alignment_features = normal_values(arg_keys[0], (ALIGNMENT_DEPTH, CHAIN_LENGTH, ALIGNMENT_WIDTH), 1.0, 6.0, ((0, 128),))
    standardize_gain = jnp.clip(1.0 + 0.15 * jax.random.normal(arg_keys[1], (ALIGNMENT_WIDTH,), jnp.float32), 0.25, 1.75)
    standardize_offset = normal_values(arg_keys[2], (ALIGNMENT_WIDTH,), 0.5, 3.0, (), jnp.float32)
    first_factor_matrix = normal_values(arg_keys[3], (ALIGNMENT_WIDTH, FACTOR_DEPTH), ALIGNMENT_WIDTH ** -0.5, 0.375)
    first_factor_offset = normal_values(arg_keys[4], (FACTOR_DEPTH,), 0.5, 3.0, (), jnp.float32)
    second_factor_matrix = normal_values(arg_keys[5], (ALIGNMENT_WIDTH, FACTOR_DEPTH), ALIGNMENT_WIDTH ** -0.5, 0.375)
    second_factor_offset = normal_values(arg_keys[6], (FACTOR_DEPTH,), 0.5, 3.0, (), jnp.float32)
    final_matrix = normal_values(arg_keys[7], (FACTOR_DEPTH * FACTOR_DEPTH, PAIR), FACTOR_DEPTH ** -0.5, 1.0)
    final_offset = normal_values(arg_keys[8], (PAIR,), 0.5, 3.0, (), jnp.float32)
    pairwise_features = normal_values(arg_keys[9], (CHAIN_LENGTH, CHAIN_LENGTH, PAIR), 1.0, 6.0, ((0, 16), (1, 8)))
    return dict(alignment_features=alignment_features, standardize_gain=standardize_gain, standardize_offset=standardize_offset, first_factor_matrix=first_factor_matrix, first_factor_offset=first_factor_offset, second_factor_matrix=second_factor_matrix, second_factor_offset=second_factor_offset, final_matrix=final_matrix, final_offset=final_offset, pairwise_features=pairwise_features)


def reference(alignment_features, standardize_gain, standardize_offset, first_factor_matrix, first_factor_offset, second_factor_matrix, second_factor_offset, final_matrix, final_offset, pairwise_features):
    given_entries = alignment_features.astype(jnp.float32)
    mean = lax.optimization_barrier(jnp.mean(given_entries, axis=-1, keepdims=True))
    centred = given_entries - mean
    variance = lax.optimization_barrier(jnp.mean(centred * centred, axis=-1, keepdims=True))
    normed = (centred / jnp.sqrt(variance + 1e-05) * standardize_gain + standardize_offset).astype(jnp.bfloat16)
    left = (jnp.einsum('src,cp->srp', normed.astype(jnp.float32), first_factor_matrix.astype(jnp.float32)) + first_factor_offset).astype(jnp.bfloat16)
    right = (jnp.einsum('src,cp->srp', normed.astype(jnp.float32), second_factor_matrix.astype(jnp.float32)) + second_factor_offset).astype(jnp.bfloat16)
    alignment_span = alignment_features.shape[0]
    chain_span = alignment_features.shape[1]
    width = left.shape[2]
    block = min(16, chain_span)
    count = chain_span // block
    left_blocks = jnp.transpose(left.reshape(alignment_span, count, block, width), (1, 0, 2, 3))
    pair_blocks = pairwise_features.reshape(count, block, chain_span, pairwise_features.shape[2])
    right_wide = right.astype(jnp.float32)

    def one_block(items):
        left_piece, pair_piece = items
        outer = jnp.einsum('sic,sje->ijce', left_piece.astype(jnp.float32), right_wide)
        outer = (outer / jnp.float32(alignment_span)).astype(jnp.bfloat16)
        flat = outer.reshape(block * chain_span, width * width)
        update = jnp.dot(flat, final_matrix, preferred_element_type=jnp.float32) + final_offset
        update = update.reshape(block, chain_span, pairwise_features.shape[2])
        return (pair_piece.astype(jnp.float32) + update).astype(jnp.bfloat16)
    result = lax.map(one_block, (left_blocks, pair_blocks))
    return result.reshape(chain_span, chain_span, pairwise_features.shape[2])
```

```python
import functools

import jax
import jax.numpy as jnp
from jax import lax
from jax.experimental import pallas as pl
from jax.experimental.pallas import tpu as pltpu
from jax.sharding import PartitionSpec as P

STREAMS = (16, 16)
STEP_ROWS = 16


def project_kernel(x_ref, gain_ref, offset_ref, weights_ref, bias_ref, right_weights_ref, right_bias_ref, out_ref, left, right, flat):
    s = pl.program_id(0)
    x = x_ref[0].astype(jnp.float32)
    mean = jnp.mean(x, axis=-1, keepdims=True)
    centred = x - mean
    variance = jnp.mean(centred * centred, axis=-1, keepdims=True)
    normed = (centred * lax.rsqrt(variance + 1e-05) * gain_ref[...] + offset_ref[...]).astype(jnp.bfloat16)
    flat[...] = jnp.dot(normed, weights_ref[...], preferred_element_type=jnp.float32) + bias_ref[...]
    group = lax.broadcasted_iota(jnp.int32, (256, 128), 1) // 32
    dense = flat[pl.ds(0, 256, stride=4), :]
    for a in range(1, 4):
        dense = jnp.where(group == a, flat[pl.ds(a, 256, stride=4), :], dense)
    left[pl.ds(s, 256, stride=8), :] = dense
    turned = lax.dot_general(
        right_weights_ref[...], normed, (((1,), (1,)), ((), ())), preferred_element_type=jnp.float32
    )
    turned = turned + right_bias_ref[...]
    for cb in range(8):
        right[cb, pl.ds(s, 32, stride=8), :] = turned[:, cb * 128 : (cb + 1) * 128]

    @pl.when(s == pl.num_programs(0) - 1)
    def _():
        for r in range(16):
            for h in range(2):
                rows = left[pl.ds((r * 16 + h * 8) * 8, 64), :].astype(jnp.bfloat16)
                out_ref[h, r * 8 : (r + 1) * 8] = rows.reshape(8, 8, 128)
        for z in range(4):
            for k in range(2):
                rows = right[z * 2 + k].astype(jnp.bfloat16)
                out_ref[k, 128 + z * 32 : 128 + (z + 1) * 32] = rows.reshape(32, 8, 128)


def project(x, gain, offset, first, first_offset, second, second_offset):
    whole = lambda *shape: pl.BlockSpec(shape, lambda s: (0,) * len(shape))
    return pl.pallas_call(
        project_kernel,
        grid=(8,),
        in_specs=[
            pl.BlockSpec((1, 1024, 256), lambda s: (s, 0, 0)),
            whole(1, 256),
            whole(1, 256),
            whole(256, 128),
            whole(1, 128),
            whole(32, 256),
            whole(32, 1),
        ],
        out_specs=whole(2, 256, 8, 128),
        out_shape=jax.ShapeDtypeStruct((2, 256, 8, 128), jnp.bfloat16),
        scratch_shapes=[
            pltpu.VMEM((2048, 128), jnp.float32),
            pltpu.VMEM((8, 256, 128), jnp.float32),
            pltpu.VMEM((1024, 128), jnp.float32),
        ],
        compiler_params=pltpu.CompilerParams(vmem_limit_bytes=32 * 2**20),
        name="project",
    )(
        x,
        gain.reshape(1, 256),
        offset.reshape(1, 256),
        jnp.tile(first, (1, 4)),
        jnp.tile(first_offset, 4).reshape(1, 128),
        second.T,
        second_offset.reshape(32, 1),
    )


def turn_kernel(x_ref, out_ref):
    for place in range(0, 16, 2):
        rows = jnp.concatenate([x_ref[dz, place + d, 0] for d in range(2) for dz in range(4)], axis=0)
        out_ref[:, place * 64 : place * 64 + 128] = jnp.transpose(rows)


def turn(gathered):
    return pl.pallas_call(
        turn_kernel,
        grid=(8,),
        in_specs=[pl.BlockSpec((4, 16, 1, 16, 128), lambda q: (0, 0, q, 0, 0))],
        out_specs=pl.BlockSpec((128, 1024), lambda q: (q, 0)),
        out_shape=jax.ShapeDtypeStruct((1024, 1024), jnp.bfloat16),
        compiler_params=pltpu.CompilerParams(vmem_limit_bytes=16 * 2**20),
        name="turn",
    )(gathered)


def steps_of(part, slot, core):
    bits = [(slot >> b) & 1 for b in range(4)]
    one = lambda lo, hi: (lo * 1) ^ (hi * 3) if core == 0 else (lo * 3) ^ (hi * 1)
    near, far = one(bits[0], bits[1]), one(bits[2], bits[3])
    dx, dy = (near, far) if part == 0 else (far, near)
    return dy * 4 + dx


def product_kernel(depth, first, last, core_ref, own_ref, other_ref, a_lo, a_hi, b_lo, b_hi, weights_ref, *refs):
    refs = list(refs)
    acc_ref = None if first else refs.pop(0)
    pair_ref, offset_ref = (refs.pop(0), refs.pop(0)) if last else (None, None)
    out_ref, left, right, outer, left_sem, right_sem = refs
    half = depth // 2
    b = pl.program_id(0)
    core = core_ref[0]
    rows = STEP_ROWS * 32
    blocks = 1024 // rows

    def left_copy(n):
        source = own_ref if n < blocks else other_ref
        return pltpu.make_async_copy(
            source.at[pl.ds((n % blocks) * rows, rows)], left.at[pl.ds(n * rows, rows)], left_sem.at[n]
        )

    def right_copy(part, slot):
        lo, hi = ((a_lo, a_hi), (b_lo, b_hi))[part]
        source = lo.at[slot] if slot < 8 else hi.at[slot - 8]
        place = jnp.where(core == 0, steps_of(part, slot, 0), steps_of(part, slot, 1))
        to = pl.multiple_of(place * 64, 64)
        return pltpu.make_async_copy(
            source, right.at[pl.ds(part * half, half), pl.ds(to, 64)], right_sem.at[part, slot]
        )

    @pl.when(b == 0)
    def _():
        left_copy(0).start()
        for part in range(2):
            for slot in range(16):
                right_copy(part, slot).start()
        for n in range(1, 2 * blocks):
            left_copy(n).start()

    for n in range(2 * blocks):

        @pl.when(b == n)
        def _():
            left_copy(n).wait()

    block = left[pl.ds(pl.multiple_of(b * rows, rows), rows), :]
    wide = 4 if half % 4 == 0 else 2
    for n in range(depth // wide):
        if (n * wide) % half == 0:

            @pl.when(b == 0)
            def _():
                for slot in range(16):
                    right_copy((n * wide) // half, slot).wait()

        channels = jnp.concatenate([right[n * wide + e] for e in range(wide)], axis=1)
        m = jnp.dot(block, channels, preferred_element_type=jnp.float32).astype(jnp.bfloat16)
        for i in range(STEP_ROWS):
            for e in range(wide):
                outer[i // 2, pl.ds((n * wide + e) * 32, 32), pl.ds((i % 2) * 128, 128)] = m[
                    i * 32 : (i + 1) * 32, e * 128 : (e + 1) * 128
                ]
    for pair in range(STEP_ROWS // 2):
        both = jnp.dot(weights_ref[...], outer[pair], preferred_element_type=jnp.float32)
        for d in range(2):
            i = pair * 2 + d
            update = both[:, d * 128 : (d + 1) * 128]
            if not first:
                update = update + acc_ref[i]
            if last:
                update = jnp.transpose(update) + offset_ref[...] + pair_ref[i].astype(jnp.float32)
            out_ref[i] = update.astype(out_ref.dtype)


def product(depth, core, own, other, pieces, weights, acc, pair, offset):
    blocks = 32 // STEP_ROWS
    tile = pl.BlockSpec(
        (STEP_ROWS, 128, 128), lambda b, core: (((b // blocks) ^ core[0]) * blocks + b % blocks, 0, 0)
    )
    anywhere = pl.BlockSpec(memory_space=pl.ANY)
    operands = [own, other, *pieces, weights]
    specs = [anywhere] * 6 + [pl.BlockSpec((128, depth * 32), lambda b, core: (0, 0))]
    if acc is not None:
        operands.append(acc)
        specs.append(tile)
    last = pair is not None
    if last:
        operands += [pair, offset]
        specs += [tile, pl.BlockSpec((1, 128), lambda b, core: (0, 0))]
    return pl.pallas_call(
        functools.partial(product_kernel, depth, acc is None, last),
        grid_spec=pltpu.PrefetchScalarGridSpec(
            num_scalar_prefetch=1,
            grid=(2 * blocks,),
            in_specs=specs,
            out_specs=tile,
            scratch_shapes=[
                pltpu.VMEM((2048, 1024), jnp.bfloat16),
                pltpu.VMEM((depth, 1024, 128), jnp.bfloat16),
                pltpu.VMEM((STEP_ROWS // 2, depth * 32, 256), jnp.bfloat16),
                pltpu.SemaphoreType.DMA((2 * blocks,)),
                pltpu.SemaphoreType.DMA((2, 16)),
            ],
        ),
        out_shape=jax.ShapeDtypeStruct((64, 128, 128), jnp.bfloat16 if last else jnp.float32),
        compiler_params=pltpu.CompilerParams(vmem_limit_bytes=40 * 2**20),
        name="product",
    )(core, *operands)


def hop(part, step, index):
    row, col = index
    y, x, core = row // 4, row % 4, col % 2
    mask = (1, 3)[(step + core) % 2]
    along_x = (step < 2) == (part == 0)
    return (y * 4 + (x ^ mask), col) if along_x else ((y ^ mask) * 4 + x, col)


def permute(value, to):
    pairs = []
    for row in range(16):
        for col in range(8):
            other = to((row, col))
            pairs.append((row * 8 + col, other[0] * 8 + other[1]))
    return lax.ppermute(value, ("row", "col"), pairs)


def pick(array, index, axis):
    return lax.dynamic_index_in_dim(array, index, axis, keepdims=False)


def per_device(
    alignment_features,
    standardize_gain,
    standardize_offset,
    first_factor_matrix,
    first_factor_offset,
    second_factor_matrix,
    second_factor_offset,
    final_matrix,
    final_offset,
    pairwise_features,
):
    row, col = lax.axis_index("row"), lax.axis_index("col")
    y, x, z, core = row // 4, row % 4, col // 2, col % 2
    projected = project(
        alignment_features,
        standardize_gain,
        standardize_offset,
        first_factor_matrix,
        first_factor_offset,
        second_factor_matrix,
        second_factor_offset,
    )
    mine = pick(projected, core, 0)
    theirs = permute(pick(projected, 1 - core, 0), lambda d: (d[0], d[1] ^ 1))
    merged = jnp.where(
        core == 0, jnp.concatenate([mine, theirs], axis=1), jnp.concatenate([theirs, mine], axis=1)
    )

    right = merged[128:].reshape(4, 32, 16, 128)
    planes = [pick(right, z, 0)] + [
        permute(pick(right, z ^ d, 0), lambda i, d=d: (i[0], ((i[1] // 2) ^ d) * 2 + i[1] % 2)) for d in (1, 2, 3)
    ]
    right = jnp.concatenate(planes, axis=1)

    left = merged[:128].reshape(4, 4, 8, 16, 128)
    left = jnp.stack(
        [pick(left, x, 1)]
        + [permute(pick(left, x ^ d, 1), lambda i, d=d: ((i[0] // 4) * 4 + ((i[0] % 4) ^ d), i[1])) for d in (1, 2, 3)]
    )
    left = jnp.stack(
        [pick(left, y, 1)]
        + [permute(pick(left, y ^ d, 1), lambda i, d=d: (((i[0] // 4) ^ d) * 4 + i[0] % 4, i[1])) for d in (1, 2, 3)]
    )

    def over_z(value, step):
        def to(i):
            mask = (1, 3)[(step + i[1] % 2) % 2]
            return i[0], ((i[1] // 2) ^ mask) * 2 + i[1] % 2

        return permute(value, to)

    near = over_z(left, 0)
    held = jnp.stack([left, near])
    far = over_z(held, 1)
    one = jnp.where(core == 0, held[1], far[0])
    three = jnp.where(core == 0, far[0], held[1])
    left = jnp.stack([left, one, far[1], three]).reshape(4, 16, 8, 16, 128)
    own = turn(left)
    other = permute(own, lambda d: (d[0], d[1] ^ 1))

    weights = (final_matrix / 1024).astype(jnp.bfloat16).reshape(32, 32, 128)
    weights = jnp.transpose(weights, (2, 1, 0))
    core_index = core.astype(jnp.int32).reshape(1)
    acc = None
    at = 0
    for n, depth in enumerate(STREAMS):
        pieces = []
        for part in range(2):
            e0 = at + part * (depth // 2)
            have = right[e0 : e0 + depth // 2][None]
            for step in range(4):
                got = permute(have, functools.partial(hop, part, step))
                if step < 3:
                    have = jnp.concatenate([have, got], axis=0)
            pieces += [have, got]
        last = n == len(STREAMS) - 1
        acc = product(
            depth,
            core_index,
            own,
            other,
            pieces,
            weights[:, at : at + depth].reshape(128, depth * 32),
            acc,
            pairwise_features if last else None,
            final_offset.reshape(1, 128) if last else None,
        )
        at += depth
    return acc


def solution(mesh):
    placed = (
        P(("row", "col"), None, None),
        P(),
        P(),
        P(),
        P(),
        P(),
        P(),
        P(),
        P(),
        P("row", "col", None),
    )
    return jax.shard_map(
        per_device, mesh=mesh, in_specs=placed, out_specs=P("row", "col", None), check_vma=False
    )
```

```python
import functools

import jax
import jax.numpy as jnp
import numpy as np
from jax import lax
from jax.experimental import pallas as pl
from jax.experimental.pallas import tpu as pltpu
from jax.sharding import PartitionSpec as P

MIB = 2**20
UNITS = [()]
for _step in range(1, 4):
    UNITS += [steps + (_step,) for steps in UNITS]
ORDER = (0,1,2,4,3,5,6,7)
PRODUCTS = ((0,2,(0,0,0,0),8000),(2,5,(2,2,2,2),12000),(5,8,(5,5,5,5),80))


def project_kernel(x_ref, gain_ref, offset_ref, first_ref, first_offset_ref, second_ref, second_offset_ref, out_ref, held, left, right, ready):
    def fetch(s):
        return pltpu.make_async_copy(x_ref.at[s], held.at[s], ready.at[s])

    for s in range(8):
        fetch(s).start()
    zeros = jnp.zeros((32, 256), jnp.bfloat16)
    first = jnp.concatenate(
        [jnp.concatenate([first_ref[...] if a == b else zeros for b in range(4)], axis=1) for a in range(4)], axis=0
    )
    first_offset = jnp.concatenate([first_offset_ref[...]] * 4, axis=1)
    diagonal = lax.broadcasted_iota(jnp.int32, (32, 32), 0) == lax.broadcasted_iota(jnp.int32, (32, 32), 1)
    second_offset = jnp.sum(jnp.where(diagonal, second_offset_ref[...], 0.0), axis=1, keepdims=True)
    contract_last = (((1,), (1,)), ((), ()))

    for s in range(8):
        for t in {0: (0,), 1: (1, 2, 3), 4: (4, 5, 6, 7)}.get(s, ()):
            fetch(t).wait()
        x = held[s].astype(jnp.float32)
        mean = jnp.mean(x, axis=-1, keepdims=True)
        centred = x - mean
        variance = jnp.mean(centred * centred, axis=-1, keepdims=True)
        normed = (centred * lax.rsqrt(variance + 1e-05) * gain_ref[...] + offset_ref[...]).astype(jnp.bfloat16)
        grouped = normed.reshape(16, 4, 16, 256)
        grouped = jnp.concatenate([grouped[:, a].reshape(256, 256) for a in range(4)], axis=1)
        dense = lax.dot_general(grouped, first, contract_last, preferred_element_type=jnp.float32)
        left[pl.ds(s, 256, stride=8), :] = dense + first_offset
        turned = lax.dot_general(second_ref[...], normed, contract_last, preferred_element_type=jnp.float32)
        turned = turned + second_offset
        for c in range(8):
            right[c, pl.ds(s, 32, stride=8), :] = turned[:, c * 128 : (c + 1) * 128]

    for r in range(16):
        rows = left[r * 128 : (r + 1) * 128, :].astype(jnp.bfloat16).reshape(8, 2, 8, 128)
        for d in range(2):
            out_ref[r, :, :, d * 128 : (d + 1) * 128] = rows[:, d]
    for c in range(8):
        rows = right[c].astype(jnp.bfloat16).reshape(16, 2, 8, 128)
        for d in range(2):
            out_ref[:, c, :, 256 + d * 128 : 256 + (d + 1) * 128] = rows[:, d]


def project(x, gain, offset, first, first_offset, second, second_offset):
    whole = pl.BlockSpec(memory_space=pltpu.VMEM)
    return pl.pallas_call(
        project_kernel,
        in_specs=[pl.BlockSpec(memory_space=pl.ANY)] + [whole] * 6,
        out_specs=whole,
        out_shape=jax.ShapeDtypeStruct((16, 8, 8, 512), jnp.bfloat16),
        scratch_shapes=[
            pltpu.VMEM((8, 1024, 256), jnp.bfloat16),
            pltpu.VMEM((2048, 128), jnp.float32),
            pltpu.VMEM((8, 256, 128), jnp.float32),
            pltpu.SemaphoreType.DMA((8,)),
        ],
        compiler_params=pltpu.CompilerParams(vmem_limit_bytes=58 * MIB),
        name="project",
    )(
        x,
        gain.reshape(1, 256),
        offset.reshape(1, 256),
        first.T,
        first_offset.reshape(1, 32),
        second.T,
        second_offset.reshape(1, 32),
    )


def split_kernel(x_ref, left_ref, right_ref):
    for n in range(8):
        at = n * 128
        left_ref[:, at : at + 128] = jnp.transpose(x_ref[at : at + 128, :256])
    for d in range(2):
        right_ref[d] = x_ref[:, 256 + d * 128 : 256 + (d + 1) * 128]


def split(received):
    return pl.pallas_call(
        split_kernel,
        out_shape=(
            jax.ShapeDtypeStruct((256, 1024), jnp.bfloat16),
            jax.ShapeDtypeStruct((2, 1024, 128), jnp.bfloat16),
        ),
        compiler_params=pltpu.CompilerParams(vmem_limit_bytes=16 * MIB),
        name="split",
    )(received)


def product_kernel(low, high, starts, last, place_ref, *refs):
    refs = list(refs)
    blocks = [b for b in range(4) if starts[b] is not None]
    left_refs = {b: (refs.pop(0), refs.pop(0)) for b in blocks}
    right_refs = [refs.pop(0) for _ in range(2 * (high - low))]
    weights_ref = refs.pop(0)
    adds = any(starts[b] for b in blocks)
    acc_ref = refs.pop(0) if adds else None
    pair_ref, offset_ref = (refs.pop(0), refs.pop(0)) if last else (None, None)
    out_ref, left, right, outer, total = refs[:5]
    refs = refs[5:]
    paired, result = (refs.pop(0), refs.pop(0)) if last else (None, None)
    left_sem, right_sem, acc_sem, pair_sem, out_sem = refs
    core = place_ref[4]

    def left_copy(b, theirs):
        rows = pl.multiple_of(b * 512 + jnp.where(core == theirs, 0, 256), 256)
        return pltpu.make_async_copy(left_refs[b][theirs], left.at[pl.ds(rows, 256)], left_sem.at[b, theirs])

    def right_copy(n):
        return pltpu.make_async_copy(right_refs[n], right.at[pl.ds(2 * n, 2)], right_sem.at[n])

    def acc_copy(b):
        return pltpu.make_async_copy(acc_ref.at[b], total.at[b], acc_sem.at[b])

    def tile(b, a):
        return pl.ds(pl.multiple_of(a * 16 + place_ref[b] * 4, 4), 4)

    def pair_copy(b, a):
        return pltpu.make_async_copy(pair_ref.at[tile(b, a)], paired.at[b, a], pair_sem.at[b, a])

    def out_copies(b):
        if last:
            return [pltpu.make_async_copy(result.at[b, a], out_ref.at[tile(b, a)], out_sem.at[b, a]) for a in range(4)]
        return [pltpu.make_async_copy(total.at[b], out_ref.at[b], out_sem.at[b, 0])]

    for b in blocks:
        for theirs in range(2):
            left_copy(b, theirs).start()
        if b == blocks[0]:
            for n in range(len(right_refs)):
                right_copy(n).start()
        if starts[b]:
            acc_copy(b).start()
        if last:
            for a in range(4):
                pair_copy(b, a).start()

    weights = weights_ref[:, low * 128 : high * 128]

    def second(b, first_unit, pairs):
        for at in pairs:
            rows = slice((first_unit - low) * 128, (high - low) * 128)
            both = jnp.dot(weights[:, rows], outer[b % 2, at, rows], preferred_element_type=jnp.float32)
            for d in range(2):
                i = at * 2 + d
                update = both[:, d * 128 : (d + 1) * 128]
                if first_unit:
                    update = update + total[b, i]
                if last:
                    a, t = i % 4, i // 4
                    update = jnp.transpose(update) + offset_ref[...] + paired[b, a, t].astype(jnp.float32)
                    result[b, a, t] = update.astype(result.dtype)
                else:
                    total[b, i] = update

    arrived = 0
    for n, b in enumerate(blocks + [None]):
        before = blocks[n - 1] if n else None
        if n == 0:
            for theirs in range(2):
                left_copy(b, theirs).wait()
        if n == 1:
            for other in blocks:
                if other != blocks[0]:
                    for theirs in range(2):
                        left_copy(other, theirs).wait()
                if starts[other]:
                    acc_copy(other).wait()
                if last:
                    for a in range(4):
                        pair_copy(other, a).wait()
        units = range(starts[b] - low, high - low) if b is not None else range(2)
        for count, unit in enumerate(units):
            if b is not None:
                while arrived <= unit or (count == len(units) - 1 and arrived < high - low):
                    right_copy(2 * arrived).wait()
                    right_copy(2 * arrived + 1).wait()
                    arrived += 1
                channels = jnp.concatenate([right[4 * unit + e] for e in range(4)], axis=1)
                m = jnp.dot(left[b * 512 : (b + 1) * 512, :], channels, preferred_element_type=jnp.float32)
                m = m.astype(jnp.bfloat16)
                for i in range(16):
                    for e in range(4):
                        at = (4 * unit + e) * 32
                        outer[b % 2, i // 2, at : at + 32, (i % 2) * 128 : (i % 2 + 1) * 128] = m[
                            i * 32 : (i + 1) * 32, e * 128 : (e + 1) * 128
                        ]
            if before is not None:
                second(before, starts[before], range(count * 8 // len(units), (count + 1) * 8 // len(units)))
        if before is not None:
            for copy in out_copies(before):
                copy.start()
    for b in blocks:
        for copy in out_copies(b):
            copy.wait()


def product(place, left, right, low, high, starts, cost, weights, acc, pair, offset):
    depth = 4 * (high - low)
    blocks = [b for b in range(4) if starts[b] is not None]
    anywhere = pl.BlockSpec(memory_space=pl.ANY)
    whole = pl.BlockSpec(memory_space=pltpu.VMEM)
    operands = [piece for b in blocks for piece in left[b]] + right
    specs = [anywhere] * len(operands) + [whole]
    operands.append(weights)
    scratch = [
        pltpu.VMEM((2048, 1024), jnp.bfloat16),
        pltpu.VMEM((depth, 1024, 128), jnp.bfloat16),
        pltpu.VMEM((2, 8, depth * 32, 256), jnp.bfloat16),
        pltpu.VMEM((4, 16, 128, 128), jnp.float32),
    ]
    if any(starts[b] for b in blocks):
        operands.append(acc)
        specs.append(anywhere)
    last = pair is not None
    if last:
        operands += [pair, offset]
        specs += [anywhere, whole]
        scratch += [pltpu.VMEM((4, 4, 4, 128, 128), jnp.bfloat16)] * 2
    return pl.pallas_call(
        functools.partial(product_kernel, low, high, starts, last),
        in_specs=[pl.BlockSpec(memory_space=pltpu.SMEM)] + specs,
        out_specs=anywhere,
        scratch_shapes=scratch
        + [
            pltpu.SemaphoreType.DMA((4, 2)),
            pltpu.SemaphoreType.DMA((len(right),)),
            pltpu.SemaphoreType.DMA((4,)),
            pltpu.SemaphoreType.DMA((4, 4)),
            pltpu.SemaphoreType.DMA((4, 4)),
        ],
        out_shape=jax.ShapeDtypeStruct((64, 128, 128), jnp.bfloat16)
        if last
        else jax.ShapeDtypeStruct((4, 16, 128, 128), jnp.float32),
        compiler_params=pltpu.CompilerParams(vmem_limit_bytes=24 * MIB),
        cost_estimate=pl.CostEstimate(flops=cost * 10**6, bytes_accessed=MIB, transcendentals=0),
        name="product",
    )(place, *operands)


def permute(value, to):
    pairs = []
    for row in range(16):
        for col in range(8):
            other = to((row, col))
            pairs.append((row * 8 + col, other[0] * 8 + other[1]))
    return lax.ppermute(value, ("row", "col"), pairs)


def mask_of(step, core):
    return (1, 3)[(step + core) % 2]


def hop(part, step, index):
    row, col = index
    y, x = row // 4, row % 4
    mask = mask_of(step, col % 2)
    along_x = (step < 2) == (part == 0)
    return (y * 4 + (x ^ mask), col) if along_x else ((y ^ mask) * 4 + x, col)


def offsets(part, steps, core):
    out = 0
    for step in steps:
        mask = mask_of(step, core)
        out ^= mask if (step < 2) == (part == 0) else mask * 4
    return out


def per_device(
    alignment_features,
    standardize_gain,
    standardize_offset,
    first_factor_matrix,
    first_factor_offset,
    second_factor_matrix,
    second_factor_offset,
    final_matrix,
    final_offset,
    pairwise_features,
):
    row, col = lax.axis_index("row"), lax.axis_index("col")
    z, core = col // 2, col % 2
    projected = project(
        alignment_features,
        standardize_gain,
        standardize_offset,
        first_factor_matrix,
        first_factor_offset,
        second_factor_matrix,
        second_factor_offset,
    ).reshape(128, 8, 512)
    received = lax.all_to_all(projected, ("row", "col"), split_axis=0, concat_axis=0, tiled=True)

    order = np.array(
        [
            [
                (offsets(part, steps + extra, which), part)
                for steps in [UNITS[unit] for unit in ORDER]
                for part in range(2)
                for extra in [(), (0,)]
            ]
            for which in range(2)
        ]
    )
    order = jnp.where(core == 0, order[0], order[1])
    channel = (row ^ order[:, 0]) * 2 + order[:, 1]
    weights = (final_matrix / 1024).astype(jnp.bfloat16).reshape(32, 32, 128)
    weights = jnp.transpose(jnp.take(weights, channel, axis=1), (2, 1, 0)).reshape(128, 1024)

    place = jnp.stack([z, z ^ 1, z ^ 3, z ^ 2, core]).astype(jnp.int32)
    received, weights, place = lax.optimization_barrier((received, weights, place))
    own, right = split(received.reshape(1024, 512))

    parts = []
    for part in range(2):
        block = right[part : part + 1]
        unit = jnp.concatenate([block, permute(block, functools.partial(hop, part, 0))], axis=0)
        units = [unit]
        for step in range(1, 4):
            units += [permute(unit, functools.partial(hop, part, step)) for unit in units]
        parts.append(units)

    over_z = lambda value, mask: permute(value, lambda i: (i[0], ((i[1] // 2) ^ mask) * 2 + i[1] % 2))
    over_z_by_core = lambda value: permute(value, lambda i: (i[0], ((i[1] // 2) ^ (3, 1)[i[1] % 2]) * 2 + i[1] % 2))
    near, far = over_z(own, 1), over_z(own, 3)
    opposite = over_z_by_core(jnp.where(core == 0, near, far))
    left = []
    for block in (own, near, far, opposite):
        left.append((block, permute(block, lambda i: (i[0], i[1] ^ 1))))

    acc = None
    for low, high, starts, cost in PRODUCTS:
        last = high == 8
        acc = product(
            place,
            left,
            [parts[part][unit] for unit in ORDER[low:high] for part in range(2)],
            low,
            high,
            starts,
            cost,
            weights,
            acc,
            pairwise_features if last else None,
            final_offset.reshape(1, 128) if last else None,
        )
    return acc


def solution(mesh):
    placed = (
        P(("row", "col"), None, None),
        P(),
        P(),
        P(),
        P(),
        P(),
        P(),
        P(),
        P(),
        P("row", "col", None),
    )
    return jax.shard_map(
        per_device, mesh=mesh, in_specs=placed, out_specs=P("row", "col", None), check_vma=False
    )
```

```python
import functools

import jax
import jax.numpy as jnp
import numpy as np
from jax import lax
from jax.experimental import pallas as pl
from jax.experimental.pallas import tpu as pltpu
from jax.sharding import PartitionSpec as P

MIB = 2**20
UNITS = [()]
for _step in range(1, 4):
    UNITS += [steps + (_step,) for steps in UNITS]
ORDER = (0,1,2,3,4,5,6,7)
TIED = 0
PRODUCTS = ((0,2,(0,0,0,None),8000),(0,6,(2,2,2,0),8000),(6,8,(6,6,6,6),80))


def project_kernel(x_ref, gain_ref, offset_ref, first_ref, first_offset_ref, second_ref, second_offset_ref, out_ref, held, left, right, ready):
    def fetch(s):
        return pltpu.make_async_copy(x_ref.at[s], held.at[s], ready.at[s])

    for s in range(8):
        fetch(s).start()
    zeros = jnp.zeros((32, 256), jnp.bfloat16)
    first = jnp.concatenate(
        [jnp.concatenate([first_ref[...] if a == b else zeros for b in range(4)], axis=1) for a in range(4)], axis=0
    )
    first_offset = jnp.concatenate([first_offset_ref[...]] * 4, axis=1)
    diagonal = lax.broadcasted_iota(jnp.int32, (32, 32), 0) == lax.broadcasted_iota(jnp.int32, (32, 32), 1)
    second_offset = jnp.sum(jnp.where(diagonal, second_offset_ref[...], 0.0), axis=1, keepdims=True)
    contract_last = (((1,), (1,)), ((), ()))

    for s in range(8):
        for t in {0: (0,), 1: (1, 2, 3), 4: (4, 5, 6, 7)}.get(s, ()):
            fetch(t).wait()
        x = held[s].astype(jnp.float32)
        mean = jnp.mean(x, axis=-1, keepdims=True)
        centred = x - mean
        variance = jnp.mean(centred * centred, axis=-1, keepdims=True)
        normed = (centred * lax.rsqrt(variance + 1e-05) * gain_ref[...] + offset_ref[...]).astype(jnp.bfloat16)
        grouped = normed.reshape(16, 4, 16, 256)
        grouped = jnp.concatenate([grouped[:, a].reshape(256, 256) for a in range(4)], axis=1)
        dense = lax.dot_general(grouped, first, contract_last, preferred_element_type=jnp.float32)
        left[pl.ds(s, 256, stride=8), :] = dense + first_offset
        turned = lax.dot_general(second_ref[...], normed, contract_last, preferred_element_type=jnp.float32)
        turned = turned + second_offset
        for c in range(8):
            right[c, pl.ds(s, 32, stride=8), :] = turned[:, c * 128 : (c + 1) * 128]

    for r in range(16):
        rows = left[r * 128 : (r + 1) * 128, :].astype(jnp.bfloat16).reshape(8, 2, 8, 128)
        for d in range(2):
            out_ref[r, :, :, d * 128 : (d + 1) * 128] = rows[:, d]
    for c in range(8):
        rows = right[c].astype(jnp.bfloat16).reshape(16, 2, 8, 128)
        for d in range(2):
            out_ref[:, c, :, 256 + d * 128 : 256 + (d + 1) * 128] = rows[:, d]


def project(x, gain, offset, first, first_offset, second, second_offset):
    whole = pl.BlockSpec(memory_space=pltpu.VMEM)
    return pl.pallas_call(
        project_kernel,
        in_specs=[pl.BlockSpec(memory_space=pl.ANY)] + [whole] * 6,
        out_specs=whole,
        out_shape=jax.ShapeDtypeStruct((16, 8, 8, 512), jnp.bfloat16),
        scratch_shapes=[
            pltpu.VMEM((8, 1024, 256), jnp.bfloat16),
            pltpu.VMEM((2048, 128), jnp.float32),
            pltpu.VMEM((8, 256, 128), jnp.float32),
            pltpu.SemaphoreType.DMA((8,)),
        ],
        compiler_params=pltpu.CompilerParams(vmem_limit_bytes=58 * MIB),
        name="project",
    )(
        x,
        gain.reshape(1, 256),
        offset.reshape(1, 256),
        first.T,
        first_offset.reshape(1, 32),
        second.T,
        second_offset.reshape(1, 32),
    )


def split_kernel(x_ref, left_ref, right_ref):
    for n in range(8):
        at = n * 128
        left_ref[:, at : at + 128] = jnp.transpose(x_ref[at : at + 128, :256])
    for d in range(2):
        right_ref[d] = x_ref[:, 256 + d * 128 : 256 + (d + 1) * 128]


def split(received):
    return pl.pallas_call(
        split_kernel,
        out_shape=(
            jax.ShapeDtypeStruct((256, 1024), jnp.bfloat16),
            jax.ShapeDtypeStruct((2, 1024, 128), jnp.bfloat16),
        ),
        compiler_params=pltpu.CompilerParams(vmem_limit_bytes=16 * MIB),
        name="split",
    )(received)


def product_kernel(low, high, right_at, starts, last, place_ref, *refs):
    refs = list(refs)
    blocks = [b for b in range(4) if starts[b] is not None]
    left_refs = {b: (refs.pop(0), refs.pop(0)) for b in blocks}
    right_refs = [refs.pop(0) for _ in range(max(index for index, _ in right_at) + 1)]
    weights_ref = refs.pop(0)
    adds = any(starts[b] for b in blocks)
    acc_ref = refs.pop(0) if adds else None
    pair_ref, offset_ref = (refs.pop(0), refs.pop(0)) if last else (None, None)
    out_ref, left, right, outer, total = refs[:5]
    refs = refs[5:]
    paired, result = (refs.pop(0), refs.pop(0)) if last else (None, None)
    left_sem, right_sem, acc_sem, pair_sem, out_sem = refs
    core = place_ref[4]

    def left_copy(b, theirs):
        rows = pl.multiple_of(b * 512 + jnp.where(core == theirs, 0, 256), 256)
        return pltpu.make_async_copy(left_refs[b][theirs], left.at[pl.ds(rows, 256)], left_sem.at[b, theirs])

    def right_copy(n):
        index, offset = right_at[n]
        source = right_refs[index].at[pl.ds(offset, 2)]
        return pltpu.make_async_copy(source, right.at[pl.ds(2 * n, 2)], right_sem.at[n])

    def acc_copy(b):
        return pltpu.make_async_copy(acc_ref.at[b], total.at[b], acc_sem.at[b])

    def tile(b, a):
        return pl.ds(pl.multiple_of(a * 16 + place_ref[b] * 4, 4), 4)

    def pair_copy(b, a):
        return pltpu.make_async_copy(pair_ref.at[tile(b, a)], paired.at[b, a], pair_sem.at[b, a])

    def out_copies(b):
        if last:
            return [pltpu.make_async_copy(result.at[b, a], out_ref.at[tile(b, a)], out_sem.at[b, a]) for a in range(4)]
        return [pltpu.make_async_copy(total.at[b], out_ref.at[b], out_sem.at[b, 0])]

    for b in blocks:
        for theirs in range(2):
            left_copy(b, theirs).start()
        if b == blocks[0]:
            for n in range(2 * (high - low)):
                right_copy(n).start()
        if starts[b]:
            acc_copy(b).start()
        if last:
            for a in range(4):
                pair_copy(b, a).start()

    weights = weights_ref[:, low * 128 : high * 128]

    def second(b, first_unit, pairs):
        for at in pairs:
            rows = slice((first_unit - low) * 128, (high - low) * 128)
            both = jnp.dot(weights[:, rows], outer[b % 2, at, rows], preferred_element_type=jnp.float32)
            for d in range(2):
                i = at * 2 + d
                update = both[:, d * 128 : (d + 1) * 128]
                if first_unit:
                    update = update + total[b, i]
                if last:
                    a, t = i % 4, i // 4
                    update = jnp.transpose(update) + offset_ref[...] + paired[b, a, t].astype(jnp.float32)
                    result[b, a, t] = update.astype(result.dtype)
                else:
                    total[b, i] = update

    arrived = 0
    for n, b in enumerate(blocks + [None]):
        before = blocks[n - 1] if n else None
        if n == 0:
            for theirs in range(2):
                left_copy(b, theirs).wait()
        if n == 1:
            for other in blocks[1:]:
                for theirs in range(2):
                    left_copy(other, theirs).wait()
        if n in (1, 2):
            for other in blocks[:1] if n == 1 else blocks[1:]:
                if starts[other]:
                    acc_copy(other).wait()
                if last:
                    for a in range(4):
                        pair_copy(other, a).wait()
        units = range(starts[b] - low, high - low) if b is not None else range(2)
        for count, unit in enumerate(units):
            if b is not None:
                while arrived <= unit or (count == len(units) - 1 and arrived < high - low):
                    right_copy(2 * arrived).wait()
                    right_copy(2 * arrived + 1).wait()
                    arrived += 1
                channels = jnp.concatenate([right[4 * unit + e] for e in range(4)], axis=1)
                m = jnp.dot(left[b * 512 : (b + 1) * 512, :], channels, preferred_element_type=jnp.float32)
                m = m.astype(jnp.bfloat16)
                for i in range(16):
                    for e in range(4):
                        at = (4 * unit + e) * 32
                        outer[b % 2, i // 2, at : at + 32, (i % 2) * 128 : (i % 2 + 1) * 128] = m[
                            i * 32 : (i + 1) * 32, e * 128 : (e + 1) * 128
                        ]
            if before is not None:
                second(before, starts[before], range(count * 8 // len(units), (count + 1) * 8 // len(units)))
        if before is not None:
            for copy in out_copies(before):
                copy.start()
    for b in blocks:
        for copy in out_copies(b):
            copy.wait()


def product(place, left, right, low, high, starts, cost, weights, acc, pair, offset):
    depth = 4 * (high - low)
    blocks = [b for b in range(4) if starts[b] is not None]
    anywhere = pl.BlockSpec(memory_space=pl.ANY)
    whole = pl.BlockSpec(memory_space=pltpu.VMEM)
    arrays, right_at = [], []
    for array, at in right:
        if not any(array is other for other in arrays):
            arrays.append(array)
        right_at.append(([array is other for other in arrays].index(True), at))
    operands = [piece for b in blocks for piece in left[b]] + arrays
    specs = [anywhere] * len(operands) + [whole]
    operands.append(weights)
    scratch = [
        pltpu.VMEM((2048, 1024), jnp.bfloat16),
        pltpu.VMEM((depth, 1024, 128), jnp.bfloat16),
        pltpu.VMEM((2, 8, depth * 32, 256), jnp.bfloat16),
        pltpu.VMEM((4, 16, 128, 128), jnp.float32),
    ]
    if any(starts[b] for b in blocks):
        operands.append(acc)
        specs.append(anywhere)
    last = pair is not None
    if last:
        operands += [pair, offset]
        specs += [anywhere, whole]
        scratch += [pltpu.VMEM((4, 4, 4, 128, 128), jnp.bfloat16)] * 2
    return pl.pallas_call(
        functools.partial(product_kernel, low, high, right_at, starts, last),
        in_specs=[pl.BlockSpec(memory_space=pltpu.SMEM)] + specs,
        out_specs=anywhere,
        scratch_shapes=scratch
        + [
            pltpu.SemaphoreType.DMA((4, 2)),
            pltpu.SemaphoreType.DMA((len(right),)),
            pltpu.SemaphoreType.DMA((4,)),
            pltpu.SemaphoreType.DMA((4, 4)),
            pltpu.SemaphoreType.DMA((4, 4)),
        ],
        out_shape=jax.ShapeDtypeStruct((64, 128, 128), jnp.bfloat16)
        if last
        else jax.ShapeDtypeStruct((4, 16, 128, 128), jnp.float32),
        compiler_params=pltpu.CompilerParams(vmem_limit_bytes=(20 if last else 26) * MIB),
        cost_estimate=pl.CostEstimate(flops=cost * 10**6, bytes_accessed=MIB, transcendentals=0),
        name="product",
    )(place, *operands)


def permute(value, to):
    pairs = []
    for row in range(16):
        for col in range(8):
            other = to((row, col))
            pairs.append((row * 8 + col, other[0] * 8 + other[1]))
    return lax.ppermute(value, ("row", "col"), pairs)


def mask_of(step, core):
    return (1, 3)[(step + core) % 2]


def hop(part, step, index):
    row, col = index
    y, x = row // 4, row % 4
    mask = mask_of(step, col % 2)
    along_x = (step < 2) == (part == 0)
    return (y * 4 + (x ^ mask), col) if along_x else ((y ^ mask) * 4 + x, col)


def offsets(part, steps, core):
    out = 0
    for step in steps:
        mask = mask_of(step, core)
        out ^= mask if (step < 2) == (part == 0) else mask * 4
    return out


def per_device(
    alignment_features,
    standardize_gain,
    standardize_offset,
    first_factor_matrix,
    first_factor_offset,
    second_factor_matrix,
    second_factor_offset,
    final_matrix,
    final_offset,
    pairwise_features,
):
    row, col = lax.axis_index("row"), lax.axis_index("col")
    z, core = col // 2, col % 2
    projected = project(
        alignment_features,
        standardize_gain,
        standardize_offset,
        first_factor_matrix,
        first_factor_offset,
        second_factor_matrix,
        second_factor_offset,
    ).reshape(128, 8, 512)
    received = lax.all_to_all(projected, ("row", "col"), split_axis=0, concat_axis=0, tiled=True)

    order = np.array(
        [
            [
                (offsets(part, steps + extra, which), part)
                for steps in [UNITS[unit] for unit in ORDER]
                for part in range(2)
                for extra in [(), (0,)]
            ]
            for which in range(2)
        ]
    )
    order = jnp.where(core == 0, order[0], order[1])
    channel = (row ^ order[:, 0]) * 2 + order[:, 1]
    weights = (final_matrix / 1024).astype(jnp.bfloat16).reshape(32, 32, 128)
    weights = jnp.transpose(jnp.take(weights, channel, axis=1), (2, 1, 0)).reshape(128, 1024)

    place = jnp.stack([z, z ^ 1, z ^ 3, z ^ 2, core]).astype(jnp.int32)
    received, weights, place = lax.optimization_barrier((received, weights, place))
    own, right = split(received.reshape(1024, 512))

    def send(blocks, step):
        return [permute(blocks[part], functools.partial(hop, part, step)) for part in range(2)]

    def join(first, second):
        return [jnp.concatenate(both, axis=0) for both in zip(first, second)]

    block = [right[part : part + 1] for part in range(2)]
    two = join(block, send(block, 0))
    two_more = send(two, 1)
    third = [send(two, 2), send(two_more, 2)]
    fourth = send(join(two, two_more), 3)

    over_z = lambda value, mask: permute(value, lambda i: (i[0], ((i[1] // 2) ^ mask) * 2 + i[1] % 2))
    over_z_by_core = lambda value: permute(value, lambda i: (i[0], ((i[1] // 2) ^ (3, 1)[i[1] % 2]) * 2 + i[1] % 2))
    near, far = over_z(own, 1), over_z(own, 3)
    opposite = over_z_by_core(jnp.where(core == 0, near, far))
    left = []
    for block in (own, near, far, opposite):
        left.append((block, permute(block, lambda i: (i[0], i[1] ^ 1))))

    acc = None
    units = [(two, 0), (two_more, 0), (third[0], 0), (third[1], 0), (fourth, 0), (fourth, 2)]
    for number, (low, high, starts, cost) in enumerate(PRODUCTS):
        last = high == 8
        acc = product(
            place,
            left,
            [(blocks[part], at) for blocks, at in units[low:high] for part in range(2)],
            low,
            high,
            starts,
            cost,
            weights,
            acc,
            pairwise_features if last else None,
            final_offset.reshape(1, 128) if last else None,
        )
        if number == TIED:
            acc, third = lax.optimization_barrier((acc, third))
            fifth = send(join(*third), 3)
            units = units[:2] + [(third[0], 0), (third[1], 0)] + units[4:] + [(fifth, 0), (fifth, 2)]
    return acc


def solution(mesh):
    placed = (
        P(("row", "col"), None, None),
        P(),
        P(),
        P(),
        P(),
        P(),
        P(),
        P(),
        P(),
        P("row", "col", None),
    )
    return jax.shard_map(
        per_device, mesh=mesh, in_specs=placed, out_specs=P("row", "col", None), check_vma=False
    )
```

```python
import functools

import jax
import jax.numpy as jnp
import numpy as np
from jax import lax
from jax.experimental import pallas as pl
from jax.experimental.pallas import tpu as pltpu
from jax.sharding import PartitionSpec as P

MIB = 2**20
UNITS = [()]
for _step in range(1, 4):
    UNITS += [steps + (_step,) for steps in UNITS]
ORDER = (0,1,2,3,4,5,6,7)
TIED = 0
PRODUCTS = ((0,2,(0,0,0,None),8000),(0,6,(2,2,2,0),8000),(6,8,(6,6,6,6),80))


def project_kernel(x_ref, gain_ref, offset_ref, first_ref, first_offset_ref, second_ref, second_offset_ref, out_ref, held, left, right, ready):
    def fetch(s):
        return pltpu.make_async_copy(x_ref.at[s], held.at[s], ready.at[s])

    for s in range(8):
        fetch(s).start()
    zeros = jnp.zeros((32, 256), jnp.bfloat16)
    first = jnp.concatenate(
        [jnp.concatenate([first_ref[...] if a == b else zeros for b in range(4)], axis=1) for a in range(4)], axis=0
    )
    first_offset = jnp.concatenate([first_offset_ref[...]] * 4, axis=1)
    diagonal = lax.broadcasted_iota(jnp.int32, (32, 32), 0) == lax.broadcasted_iota(jnp.int32, (32, 32), 1)
    second_offset = jnp.sum(jnp.where(diagonal, second_offset_ref[...], 0.0), axis=1, keepdims=True)
    contract_last = (((1,), (1,)), ((), ()))

    for s in range(8):
        for t in {0: (0,), 1: (1, 2, 3), 4: (4, 5, 6, 7)}.get(s, ()):
            fetch(t).wait()
        x = held[s].astype(jnp.float32)
        mean = jnp.mean(x, axis=-1, keepdims=True)
        centred = x - mean
        variance = jnp.mean(centred * centred, axis=-1, keepdims=True)
        normed = (centred * lax.rsqrt(variance + 1e-05) * gain_ref[...] + offset_ref[...]).astype(jnp.bfloat16)
        grouped = normed.reshape(16, 4, 16, 256)
        grouped = jnp.concatenate([grouped[:, a].reshape(256, 256) for a in range(4)], axis=1)
        dense = lax.dot_general(grouped, first, contract_last, preferred_element_type=jnp.float32)
        left[pl.ds(s, 256, stride=8), :] = dense + first_offset
        turned = lax.dot_general(second_ref[...], normed, contract_last, preferred_element_type=jnp.float32)
        turned = turned + second_offset
        for c in range(8):
            right[c, pl.ds(s, 32, stride=8), :] = turned[:, c * 128 : (c + 1) * 128]

    for r in range(16):
        rows = left[r * 128 : (r + 1) * 128, :].astype(jnp.bfloat16).reshape(8, 2, 8, 128)
        for d in range(2):
            out_ref[r, :, :, d * 128 : (d + 1) * 128] = rows[:, d]
    for c in range(8):
        rows = right[c].astype(jnp.bfloat16).reshape(16, 2, 8, 128)
        for d in range(2):
            at = 256 + d * 256
            partner = mask_of(0, c % 2) * (4 if d else 1)
            out_ref[:, c, :, at : at + 128] = rows[:, d]
            out_ref[:, c, :, at + 128 : at + 256] = jnp.stack([rows[r ^ partner, d] for r in range(16)])


def project(x, gain, offset, first, first_offset, second, second_offset):
    whole = pl.BlockSpec(memory_space=pltpu.VMEM)
    return pl.pallas_call(
        project_kernel,
        in_specs=[pl.BlockSpec(memory_space=pl.ANY)] + [whole] * 6,
        out_specs=whole,
        out_shape=jax.ShapeDtypeStruct((16, 8, 8, 768), jnp.bfloat16),
        scratch_shapes=[
            pltpu.VMEM((8, 1024, 256), jnp.bfloat16),
            pltpu.VMEM((2048, 128), jnp.float32),
            pltpu.VMEM((8, 256, 128), jnp.float32),
            pltpu.SemaphoreType.DMA((8,)),
        ],
        compiler_params=pltpu.CompilerParams(vmem_limit_bytes=58 * MIB),
        name="project",
    )(
        x,
        gain.reshape(1, 256),
        offset.reshape(1, 256),
        first.T,
        first_offset.reshape(1, 32),
        second.T,
        second_offset.reshape(1, 32),
    )


def split_kernel(x_ref, left_ref, *right_refs):
    for n in range(8):
        at = n * 128
        left_ref[:, at : at + 128] = jnp.transpose(x_ref[at : at + 128, :256])
    for n in range(4):
        right_refs[n // 2][n % 2] = x_ref[:, 256 + n * 128 : 256 + (n + 1) * 128]


def split(received):
    return pl.pallas_call(
        split_kernel,
        out_shape=(
            jax.ShapeDtypeStruct((256, 1024), jnp.bfloat16),
            jax.ShapeDtypeStruct((2, 1024, 128), jnp.bfloat16),
            jax.ShapeDtypeStruct((2, 1024, 128), jnp.bfloat16),
        ),
        compiler_params=pltpu.CompilerParams(vmem_limit_bytes=16 * MIB),
        name="split",
    )(received)


def product_kernel(low, high, right_at, starts, last, place_ref, *refs):
    refs = list(refs)
    blocks = [b for b in range(4) if starts[b] is not None]
    left_refs = {b: (refs.pop(0), refs.pop(0)) for b in blocks}
    right_refs = [refs.pop(0) for _ in range(max(index for index, _ in right_at) + 1)]
    weights_ref = refs.pop(0)
    adds = any(starts[b] for b in blocks)
    acc_ref = refs.pop(0) if adds else None
    pair_ref, offset_ref = (refs.pop(0), refs.pop(0)) if last else (None, None)
    out_ref, left, right, outer, total = refs[:5]
    refs = refs[5:]
    paired, result = (refs.pop(0), refs.pop(0)) if last else (None, None)
    left_sem, right_sem, acc_sem, pair_sem, out_sem = refs
    core = place_ref[4]

    def left_copy(b, theirs):
        rows = pl.multiple_of(b * 512 + jnp.where(core == theirs, 0, 256), 256)
        return pltpu.make_async_copy(left_refs[b][theirs], left.at[pl.ds(rows, 256)], left_sem.at[b, theirs])

    def right_copy(n):
        index, offset = right_at[n]
        source = right_refs[index].at[pl.ds(offset, 2)]
        return pltpu.make_async_copy(source, right.at[pl.ds(2 * n, 2)], right_sem.at[n])

    def acc_copy(b):
        return pltpu.make_async_copy(acc_ref.at[b], total.at[b], acc_sem.at[b])

    def tile(b, a):
        return pl.ds(pl.multiple_of(a * 16 + place_ref[b] * 4, 4), 4)

    def pair_copy(b, a):
        return pltpu.make_async_copy(pair_ref.at[tile(b, a)], paired.at[b, a], pair_sem.at[b, a])

    def out_copies(b):
        if last:
            return [pltpu.make_async_copy(result.at[b, a], out_ref.at[tile(b, a)], out_sem.at[b, a]) for a in range(4)]
        return [pltpu.make_async_copy(total.at[b], out_ref.at[b], out_sem.at[b, 0])]

    for b in blocks:
        for theirs in range(2):
            left_copy(b, theirs).start()
        if b == blocks[0]:
            for n in range(2 * (high - low)):
                right_copy(n).start()
        if starts[b]:
            acc_copy(b).start()
        if last:
            for a in range(4):
                pair_copy(b, a).start()

    weights = weights_ref[:, low * 128 : high * 128]

    def second(b, first_unit, pairs):
        for at in pairs:
            rows = slice((first_unit - low) * 128, (high - low) * 128)
            both = jnp.dot(weights[:, rows], outer[b % 2, at, rows], preferred_element_type=jnp.float32)
            for d in range(2):
                i = at * 2 + d
                update = both[:, d * 128 : (d + 1) * 128]
                if first_unit:
                    update = update + total[b, i]
                if last:
                    a, t = i % 4, i // 4
                    update = jnp.transpose(update) + offset_ref[...] + paired[b, a, t].astype(jnp.float32)
                    result[b, a, t] = update.astype(result.dtype)
                else:
                    total[b, i] = update

    arrived = 0
    for n, b in enumerate(blocks + [None]):
        before = blocks[n - 1] if n else None
        if n == 0:
            for theirs in range(2):
                left_copy(b, theirs).wait()
        if n == 1:
            for other in blocks[1:]:
                for theirs in range(2):
                    left_copy(other, theirs).wait()
        if n in (1, 2):
            for other in blocks[:1] if n == 1 else blocks[1:]:
                if starts[other]:
                    acc_copy(other).wait()
                if last:
                    for a in range(4):
                        pair_copy(other, a).wait()
        units = range(starts[b] - low, high - low) if b is not None else range(2)
        for count, unit in enumerate(units):
            if b is not None:
                while arrived <= unit or (count == len(units) - 1 and arrived < high - low):
                    right_copy(2 * arrived).wait()
                    right_copy(2 * arrived + 1).wait()
                    arrived += 1
                channels = jnp.concatenate([right[4 * unit + e] for e in range(4)], axis=1)
                m = jnp.dot(left[b * 512 : (b + 1) * 512, :], channels, preferred_element_type=jnp.float32)
                m = m.astype(jnp.bfloat16)
                for i in range(16):
                    for e in range(4):
                        at = (4 * unit + e) * 32
                        outer[b % 2, i // 2, at : at + 32, (i % 2) * 128 : (i % 2 + 1) * 128] = m[
                            i * 32 : (i + 1) * 32, e * 128 : (e + 1) * 128
                        ]
            if before is not None:
                second(before, starts[before], range(count * 8 // len(units), (count + 1) * 8 // len(units)))
        if before is not None:
            for copy in out_copies(before):
                copy.start()
    for b in blocks:
        for copy in out_copies(b):
            copy.wait()


def product(place, left, right, low, high, starts, cost, weights, acc, pair, offset):
    depth = 4 * (high - low)
    blocks = [b for b in range(4) if starts[b] is not None]
    anywhere = pl.BlockSpec(memory_space=pl.ANY)
    whole = pl.BlockSpec(memory_space=pltpu.VMEM)
    arrays, right_at = [], []
    for array, at in right:
        if not any(array is other for other in arrays):
            arrays.append(array)
        right_at.append(([array is other for other in arrays].index(True), at))
    operands = [piece for b in blocks for piece in left[b]] + arrays
    specs = [anywhere] * len(operands) + [whole]
    operands.append(weights)
    scratch = [
        pltpu.VMEM((2048, 1024), jnp.bfloat16),
        pltpu.VMEM((depth, 1024, 128), jnp.bfloat16),
        pltpu.VMEM((2, 8, depth * 32, 256), jnp.bfloat16),
        pltpu.VMEM((4, 16, 128, 128), jnp.float32),
    ]
    if any(starts[b] for b in blocks):
        operands.append(acc)
        specs.append(anywhere)
    last = pair is not None
    if last:
        operands += [pair, offset]
        specs += [anywhere, whole]
        scratch += [pltpu.VMEM((4, 4, 4, 128, 128), jnp.bfloat16)] * 2
    return pl.pallas_call(
        functools.partial(product_kernel, low, high, right_at, starts, last),
        in_specs=[pl.BlockSpec(memory_space=pltpu.SMEM)] + specs,
        out_specs=anywhere,
        scratch_shapes=scratch
        + [
            pltpu.SemaphoreType.DMA((4, 2)),
            pltpu.SemaphoreType.DMA((len(right),)),
            pltpu.SemaphoreType.DMA((4,)),
            pltpu.SemaphoreType.DMA((4, 4)),
            pltpu.SemaphoreType.DMA((4, 4)),
        ],
        out_shape=jax.ShapeDtypeStruct((64, 128, 128), jnp.bfloat16)
        if last
        else jax.ShapeDtypeStruct((4, 16, 128, 128), jnp.float32),
        compiler_params=pltpu.CompilerParams(vmem_limit_bytes=(20 if last else 26) * MIB),
        cost_estimate=pl.CostEstimate(flops=cost * 10**6, bytes_accessed=MIB, transcendentals=0),
        name="product",
    )(place, *operands)


def permute(value, to):
    pairs = []
    for row in range(16):
        for col in range(8):
            other = to((row, col))
            pairs.append((row * 8 + col, other[0] * 8 + other[1]))
    return lax.ppermute(value, ("row", "col"), pairs)


def mask_of(step, core):
    return (1, 3)[(step + core) % 2]


def hop(part, step, index):
    row, col = index
    y, x = row // 4, row % 4
    mask = mask_of(step, col % 2)
    along_x = (step < 2) == (part == 0)
    return (y * 4 + (x ^ mask), col) if along_x else ((y ^ mask) * 4 + x, col)


def offsets(part, steps, core):
    out = 0
    for step in steps:
        mask = mask_of(step, core)
        out ^= mask if (step < 2) == (part == 0) else mask * 4
    return out


def per_device(
    alignment_features,
    standardize_gain,
    standardize_offset,
    first_factor_matrix,
    first_factor_offset,
    second_factor_matrix,
    second_factor_offset,
    final_matrix,
    final_offset,
    pairwise_features,
):
    row, col = lax.axis_index("row"), lax.axis_index("col")
    z, core = col // 2, col % 2
    projected = project(
        alignment_features,
        standardize_gain,
        standardize_offset,
        first_factor_matrix,
        first_factor_offset,
        second_factor_matrix,
        second_factor_offset,
    ).reshape(128, 8, 768)
    received = lax.all_to_all(projected, ("row", "col"), split_axis=0, concat_axis=0, tiled=True)

    order = np.array(
        [
            [
                (offsets(part, steps + extra, which), part)
                for steps in [UNITS[unit] for unit in ORDER]
                for part in range(2)
                for extra in [(), (0,)]
            ]
            for which in range(2)
        ]
    )
    order = jnp.where(core == 0, order[0], order[1])
    channel = (row ^ order[:, 0]) * 2 + order[:, 1]
    weights = (final_matrix / 1024).astype(jnp.bfloat16).reshape(32, 32, 128)
    weights = jnp.transpose(jnp.take(weights, channel, axis=1), (2, 1, 0)).reshape(128, 1024)

    place = jnp.stack([z, z ^ 1, z ^ 3, z ^ 2, core]).astype(jnp.int32)
    received, weights, place = lax.optimization_barrier((received, weights, place))
    own, *two = split(received.reshape(1024, 768))

    def send(blocks, step):
        return [permute(blocks[part], functools.partial(hop, part, step)) for part in range(2)]

    def join(first, second):
        return [jnp.concatenate(both, axis=0) for both in zip(first, second)]

    two_more = send(two, 1)
    third = [send(two, 2), send(two_more, 2)]
    fourth = send(join(two, two_more), 3)

    over_z = lambda value, mask: permute(value, lambda i: (i[0], ((i[1] // 2) ^ mask) * 2 + i[1] % 2))
    over_z_by_core = lambda value: permute(value, lambda i: (i[0], ((i[1] // 2) ^ (3, 1)[i[1] % 2]) * 2 + i[1] % 2))
    near, far = over_z(own, 1), over_z(own, 3)
    opposite = over_z_by_core(jnp.where(core == 0, near, far))
    left = []
    for block in (own, near, far, opposite):
        left.append((block, permute(block, lambda i: (i[0], i[1] ^ 1))))

    acc = None
    units = [(two, 0), (two_more, 0), (third[0], 0), (third[1], 0), (fourth, 0), (fourth, 2)]
    for number, (low, high, starts, cost) in enumerate(PRODUCTS):
        last = high == 8
        acc = product(
            place,
            left,
            [(blocks[part], at) for blocks, at in units[low:high] for part in range(2)],
            low,
            high,
            starts,
            cost,
            weights,
            acc,
            pairwise_features if last else None,
            final_offset.reshape(1, 128) if last else None,
        )
        if number == TIED:
            acc, third = lax.optimization_barrier((acc, third))
            fifth = send(join(*third), 3)
            units = units[:2] + [(third[0], 0), (third[1], 0)] + units[4:] + [(fifth, 0), (fifth, 2)]
    return acc


def solution(mesh):
    placed = (
        P(("row", "col"), None, None),
        P(),
        P(),
        P(),
        P(),
        P(),
        P(),
        P(),
        P(),
        P("row", "col", None),
    )
    return jax.shard_map(
        per_device, mesh=mesh, in_specs=placed, out_specs=P("row", "col", None), check_vma=False
    )
```
